32 devices in a mesh: seq: 16 (over z, x, core), fsdp: 2 (over y).
Axes of the slice: x: 2, y: 2, z: 4, core: 2. Of those that a mesh axis runs over, the one named last changes fastest.
Arguments:
- inputs: bfloat16 [2, 128, 16, 4096], P('fsdp', None, 'seq'), may hold values from -6 to 6
- queries: bfloat16 [2, 128, 16, 4096], P('fsdp', None, 'seq'), may hold values from -1000 to 1000
- rotated_keys: bfloat16 [2, 128, 16, 512], P('fsdp', None, 'seq'), may hold values from -6 to 6
- out_grad: bfloat16 [2, 128, 16, 4096], P('fsdp', None, 'seq'), may hold values from -6 to 6
- value_weight: bfloat16 [4096, 512], P(('seq', 'fsdp')), may hold values from -0.09375 to 0.09375
- fisher: float32 [4096, 512], P(('seq', 'fsdp')), may hold values from 0.2 to 20
- anchor: float32 [4096, 512], P(('seq', 'fsdp')), may hold values from -0.25 to 0.25
- doc_starts: int32 [2, 32], P('fsdp'), may hold values from 0 to 2032, as said below
- owners: int32 [2, 32], P('fsdp'), may hold values from 0 to 15, as said below
Outputs:
- query_grad: bfloat16 [2, 16, 12, 16, 4096], P('fsdp', 'seq')
- key_grad: bfloat16 [2, 128, 16, 512], P('fsdp', None, 'seq')
- input_grad: bfloat16 [2, 128, 16, 4096], P('fsdp', None, 'seq')
- ewc_grad: float32 [4096, 512], P(('seq', 'fsdp'))
The draws below stay inside these ranges and needn't reach their ends.
Inputs may be any that keep to these rules, and one draw needn't show every extreme that they name: `doc_starts`: in each sequence the starts rise strictly from 0; every document's length (2048 minus the last start for the last one) is a multiple of 16. Each of the 16 owners is named by exactly two documents of a sequence; one owner's documents hold at most 192 positions in all, and in every sequence some owner holds exactly that many.
All inputs are finite; a program needn't handle non-finite values.
Results may differ from the reference program's by a relative error of at most 0.029.
Values may be sent and summed in bfloat16 or wider, within the bound.
A program may use at most 128 MiB of HBM per device.

```python
import math
import jax
import jax.numpy as jnp
from jax import lax

D = 4096
HEADS = 32
KVH = 4
HD = 128
TOK_DEV = 128
QW = 4096
KVW = 512
CAP = 12
SEQS = 2
TOKENS = 4096
N_SEQ = 16


def plan_sequence(key):
    lane_count = N_SEQ
    star_key, fill_key, split_key, order_key = jax.random.split(key, 4)
    star = jax.random.randint(star_key, (), 0, lane_count)
    lane_ids = jnp.arange(lane_count, dtype=jnp.int32)
    loads = jnp.where(lane_ids == star, CAP, 2).astype(jnp.int32)
    spare = TOK_DEV - 2 * (lane_count - 1) - CAP

    def add_unit(step_index, current):
        ranking = jax.random.randint(jax.random.fold_in(fill_key, step_index), (lane_count,), 0, 1 << 20) * lane_count + lane_ids
        open_lane = (current < CAP) & (lane_ids != star)
        ranking = jnp.where(open_lane, ranking, -1)
        chosen = jnp.argmax(ranking)
        return current + (lane_ids == chosen).astype(jnp.int32)
    loads = lax.fori_loop(0, spare, add_unit, loads)
    first_part = 1 + jax.random.randint(split_key, (lane_count,), 0, 1 << 20) % (loads - 1)
    doc_lengths = jnp.concatenate([first_part, loads - first_part])
    owner_ids = jnp.concatenate([lane_ids, lane_ids])
    order = jax.random.permutation(order_key, 2 * lane_count)
    doc_lengths = doc_lengths[order]
    owner_ids = owner_ids[order]
    starts = (jnp.cumsum(doc_lengths) - doc_lengths) * lane_count
    return (starts.astype(jnp.int32), owner_ids.astype(jnp.int32))


def plan_all(key):
    seq_keys = jax.random.split(jax.random.fold_in(key, 7), SEQS)
    return jax.vmap(plan_sequence)(seq_keys)


def draw_doc_starts(key, part):
    return plan_all(key)[0]


def draw_owners(key, part):
    return plan_all(key)[1]


def draw_queries(key, part):
    base_key = jax.random.fold_in(jax.random.fold_in(key, 11), 0)
    head_shape = (SEQS, TOK_DEV, N_SEQ, HEADS, HD)
    values = jax.random.normal(base_key, head_shape, jnp.float32)
    values = jnp.clip(values, -1000.0, 1000.0)
    return values.reshape(SEQS, TOK_DEV, N_SEQ, HEADS * HD).astype(jnp.bfloat16)


def level_of(key, shape, pieces, smallest, high):
    level = 1.0
    for axis_at, blocks in pieces:
        draws = jax.random.uniform(jax.random.fold_in(jax.random.fold_in(key, 6), axis_at), (blocks,), jnp.float32, smallest / len(pieces), high / len(pieces))
        level = level * jnp.repeat(jnp.exp(draws), shape[axis_at] // blocks).reshape((-1,) + (1,) * (len(shape) - 1 - axis_at))
    return level


def noise(stream_key, extent, scale, bound, pieces=(), kind=jnp.bfloat16):
    result = jax.random.normal(stream_key, extent, jnp.float32) * scale
    if len(pieces) > 0:
        result = level_of(stream_key, extent, pieces, -0.22, 0.18) * result
    return jnp.clip(result, min=-bound, max=bound).astype(kind)


def setup_inputs(seed: int = 0) -> dict:
    splits = jax.random.split(jax.random.key(seed), 10)
    inputs = noise(splits[0], (SEQS, TOK_DEV, N_SEQ, D), 1.0, 6.0, ((0, 2), (2, 16)))
    queries = draw_queries(jax.random.fold_in(splits[9], 71), 0)
    rotated_keys = noise(splits[2], (SEQS, TOK_DEV, N_SEQ, KVW), 1.0, 6.0, ((0, 2), (2, 16)))
    out_grad = noise(splits[3], (SEQS, TOK_DEV, N_SEQ, QW), 1.0, 6.0, ((0, 2), (2, 16)))
    value_weight = noise(splits[4], (D, KVW), D ** -0.5, 0.09375, ((0, 32),))
    fisher = jnp.clip(jnp.exp(math.log(20.0) - 4.6051702 * jax.random.uniform(splits[5], (D, KVW), jnp.float32) ** level_of(splits[5], (D, KVW), ((0, 32),), -0.2, 0.2)), 0.2, 20.0)
    anchor = noise(splits[6], (D, KVW), 0.015625, 0.25, ((0, 32),), jnp.float32)
    doc_starts = draw_doc_starts(jax.random.fold_in(splits[9], 71), 0)
    owners = draw_owners(jax.random.fold_in(splits[9], 71), 0)
    return dict(inputs=inputs, queries=queries, rotated_keys=rotated_keys, out_grad=out_grad, value_weight=value_weight, fisher=fisher, anchor=anchor, doc_starts=doc_starts, owners=owners)


SCORE_NEG = -1e+30
EWC_LAMBDA = 4.0

def round_plan(starts, owner_list, lane_count, rounds):
    round_ids = jnp.arange(rounds, dtype=jnp.int32)
    start_rounds = starts // lane_count
    doc_of = lax.optimization_barrier(jnp.sum((start_rounds[None, :] <= round_ids[:, None]).astype(jnp.int32), axis=1)) - 1
    doc_ids = jnp.arange(starts.shape[0], dtype=jnp.int32)
    onehot = (doc_of[:, None] == doc_ids[None, :]).astype(jnp.int32)
    owner_of = lax.optimization_barrier(jnp.sum(onehot * owner_list[None, :], axis=1))
    earlier = (owner_of[:, None] == owner_of[None, :]) & (round_ids[None, :] < round_ids[:, None])
    rank_of = lax.optimization_barrier(jnp.sum(earlier.astype(jnp.int32), axis=1))
    return (doc_of, owner_of, rank_of)

def slot_rounds(owner_of, rank_of, lane_count, capacity):
    lane_ids = jnp.arange(lane_count, dtype=jnp.int32)
    slot_ids = jnp.arange(capacity, dtype=jnp.int32)
    round_ids = jnp.arange(owner_of.shape[0], dtype=jnp.int32)
    match = (owner_of[None, None, :] == lane_ids[None, :, None]) & (rank_of[None, None, :] == slot_ids[:, None, None])
    source = lax.optimization_barrier(jnp.sum(match.astype(jnp.int32) * round_ids[None, None, :], axis=2))
    filled = jnp.any(match, axis=2)
    return (source, filled)

def one_sequence(token_in, query_in, key_in, grad_in, starts, owner_list, weight):
    length = TOK_DEV * N_SEQ
    block_rows = 128
    reach = CAP * N_SEQ
    width = block_rows + reach
    group = HEADS // KVH
    scale = 1.0 / math.sqrt(HD)
    token_flat = token_in.reshape(length, D)
    query_flat = query_in.reshape(length, HEADS * HD)
    key_flat = key_in.reshape(length, KVH * HD)
    grad_flat = grad_in.reshape(length, HEADS * HD)
    value_flat = jnp.dot(token_flat, weight, preferred_element_type=jnp.float32).astype(jnp.bfloat16)
    positions = jnp.arange(length, dtype=jnp.int32)
    doc_pos = lax.optimization_barrier(jnp.sum((starts[None, :] <= positions[:, None]).astype(jnp.int32), axis=1)) - 1

    def step(carry, block):
        key_acc, value_acc = carry
        q_start = (block * block_rows).astype(jnp.int32)
        k_start = jnp.maximum(q_start - reach, 0).astype(jnp.int32)
        q_blk = lax.dynamic_slice_in_dim(query_flat, q_start, block_rows, 0).reshape(block_rows, KVH, group, HD).astype(jnp.float32)
        g_blk = lax.dynamic_slice_in_dim(grad_flat, q_start, block_rows, 0).reshape(block_rows, KVH, group, HD).astype(jnp.float32)
        k_blk = lax.dynamic_slice_in_dim(key_flat, k_start, width, 0).reshape(width, KVH, HD).astype(jnp.float32)
        v_blk = lax.dynamic_slice_in_dim(value_flat, k_start, width, 0).reshape(width, KVH, HD).astype(jnp.float32)
        q_doc = lax.dynamic_slice_in_dim(doc_pos, q_start, block_rows, 0)
        k_doc = lax.dynamic_slice_in_dim(doc_pos, k_start, width, 0)
        q_pos = q_start + jnp.arange(block_rows, dtype=jnp.int32)
        k_pos = k_start + jnp.arange(width, dtype=jnp.int32)
        visible = (q_doc[:, None] == k_doc[None, :]) & (k_pos[None, :] <= q_pos[:, None])
        scores = jnp.einsum('qhgd,khd->hgqk', q_blk, k_blk) * scale
        masked = jnp.where(visible, scores, SCORE_NEG)
        peak = lax.optimization_barrier(jnp.max(masked, axis=3, keepdims=True))
        probs = jnp.where(visible, jnp.exp(masked - peak), 0.0)
        probs = probs / lax.optimization_barrier(jnp.sum(probs, axis=3, keepdims=True))
        probs_b = lax.optimization_barrier(probs.astype(jnp.bfloat16)).astype(jnp.float32)
        attn_out = jnp.einsum('hgqk,khd->qhgd', probs_b, v_blk)
        attn_out = lax.optimization_barrier(attn_out.astype(jnp.bfloat16)).astype(jnp.float32)
        delta = jnp.einsum('qhgd,qhgd->hgq', g_blk, attn_out)
        dprobs = jnp.einsum('qhgd,khd->hgqk', g_blk, v_blk)
        dscores = probs * (dprobs - delta[..., None]) * scale
        dscores = lax.optimization_barrier(dscores.astype(jnp.bfloat16)).astype(jnp.float32)
        query_part = jnp.einsum('hgqk,khd->qhgd', dscores, k_blk).astype(jnp.bfloat16).reshape(block_rows, HEADS * HD)
        key_part = jnp.einsum('hgqk,qhgd->khd', dscores, q_blk).reshape(width, KVH * HD)
        value_part = jnp.einsum('hgqk,qhgd->khd', probs_b, g_blk).reshape(width, KVH * HD)
        key_acc = lax.dynamic_update_slice_in_dim(key_acc, lax.dynamic_slice_in_dim(key_acc, k_start, width, 0) + key_part, k_start, 0)
        value_acc = lax.dynamic_update_slice_in_dim(value_acc, lax.dynamic_slice_in_dim(value_acc, k_start, width, 0) + value_part, k_start, 0)
        return ((key_acc, value_acc), query_part)
    blocks = jnp.arange(length // block_rows, dtype=jnp.int32)
    zeros_kv = jnp.zeros((length, KVH * HD), jnp.float32)
    (key_acc, value_acc), query_parts = lax.scan(step, (zeros_kv, zeros_kv), blocks)
    query_home = query_parts.reshape(length, HEADS * HD)
    key_grad = key_acc.astype(jnp.bfloat16)
    value_grad = value_acc.astype(jnp.bfloat16)
    input_grad = jnp.dot(value_grad, weight.T, preferred_element_type=jnp.float32).astype(jnp.bfloat16)
    partial_sum = jnp.dot(token_flat.T, value_grad, preferred_element_type=jnp.float32)
    doc_of, owner_of, rank_of = round_plan(starts, owner_list, N_SEQ, TOK_DEV)
    source, filled = slot_rounds(owner_of, rank_of, N_SEQ, CAP)
    query_rounds = query_home.reshape(TOK_DEV, N_SEQ, HEADS * HD)
    picked = jnp.take(query_rounds, source.T.reshape(-1), axis=0).reshape(N_SEQ, CAP, N_SEQ, HEADS * HD)
    query_slots = jnp.where(filled.T[:, :, None, None], picked, jnp.zeros_like(picked))
    return (query_slots, key_grad.reshape(TOK_DEV, N_SEQ, KVH * HD), input_grad.reshape(TOK_DEV, N_SEQ, D), partial_sum)

def reference(inputs, queries, rotated_keys, out_grad, value_weight, fisher, anchor, doc_starts, owners):

    def per_sequence(carry, index):
        results = one_sequence(inputs[index], queries[index], rotated_keys[index], out_grad[index], doc_starts[index], owners[index], value_weight)
        return (carry + results[3], (results[0], results[1], results[2]))
    seq_ids = jnp.arange(SEQS, dtype=jnp.int32)
    weight_sum, outs = lax.scan(per_sequence, jnp.zeros((D, KVH * HD), jnp.float32), seq_ids)
    grad_scale = 1.0 / math.sqrt(TOKENS)
    ewc_grad = weight_sum * grad_scale + EWC_LAMBDA * fisher * (value_weight.astype(jnp.float32) - anchor)
    return (outs[0], outs[1], outs[2], ewc_grad)
```

```python
import math

import jax
import jax.numpy as jnp
from jax import lax
from jax.sharding import PartitionSpec as P

KVH = 4
HD = 128


SCORE_NEG = -1e30
EWC_LAMBDA = 4.0


def round_plan(starts, owner_list, lane_count, rounds):
    round_ids = jnp.arange(rounds, dtype=jnp.int32)
    start_rounds = starts // lane_count
    doc_of = jnp.sum((start_rounds[None, :] <= round_ids[:, None]).astype(jnp.int32), axis=1) - 1
    doc_ids = jnp.arange(starts.shape[0], dtype=jnp.int32)
    onehot = (doc_of[:, None] == doc_ids[None, :]).astype(jnp.int32)
    owner_of = jnp.sum(onehot * owner_list[None, :], axis=1)
    earlier = (owner_of[:, None] == owner_of[None, :]) & (round_ids[None, :] < round_ids[:, None])
    rank_of = jnp.sum(earlier.astype(jnp.int32), axis=1)
    return (doc_of, owner_of, rank_of)


def slot_rounds(owner_of, rank_of, lane_count, capacity):
    lane_ids = jnp.arange(lane_count, dtype=jnp.int32)
    slot_ids = jnp.arange(capacity, dtype=jnp.int32)
    round_ids = jnp.arange(owner_of.shape[0], dtype=jnp.int32)
    match = (owner_of[None, None, :] == lane_ids[None, :, None]) & (
        rank_of[None, None, :] == slot_ids[:, None, None]
    )
    source = jnp.sum(match.astype(jnp.int32) * round_ids[None, None, :], axis=2)
    filled = jnp.any(match, axis=2)
    return (source, filled)


def attend(query_in, grad_in, key_in, value_in, visible):
    slot_count = query_in.shape[0] * query_in.shape[1]
    group = query_in.shape[3] // HD
    scale = 1.0 / math.sqrt(HD)
    query_parts = []
    key_parts = []
    value_parts = []
    for item_index in range(query_in.shape[2]):
        q_item = query_in[:, :, item_index, :].reshape(slot_count, group, HD)
        g_item = grad_in[:, :, item_index, :].reshape(slot_count, group, HD)
        k_item = key_in[:, :, item_index, :].reshape(slot_count, HD)
        v_item = value_in[:, :, item_index, :].reshape(slot_count, HD)
        scores = (
            jnp.einsum("mgd,kd->gmk", q_item, k_item, preferred_element_type=jnp.float32) * scale
        )
        masked = jnp.where(visible[None], scores, SCORE_NEG)
        peak = jnp.max(masked, axis=2, keepdims=True)
        probs = jnp.where(visible[None], jnp.exp(masked - peak), 0.0)
        totals = jnp.sum(probs, axis=2, keepdims=True)
        probs = probs / jnp.where(totals > 0.0, totals, 1.0)
        probs_b = probs.astype(jnp.bfloat16)
        attn_out = jnp.einsum(
            "gmk,kd->mgd", probs_b, v_item, preferred_element_type=jnp.float32
        ).astype(jnp.bfloat16)
        delta = jnp.einsum("mgd,mgd->gm", g_item, attn_out, preferred_element_type=jnp.float32)
        dprobs = jnp.einsum("mgd,kd->gmk", g_item, v_item, preferred_element_type=jnp.float32)
        dscores = (probs * (dprobs - delta[:, :, None]) * scale).astype(jnp.bfloat16)
        query_grad = jnp.einsum(
            "gmk,kd->mgd", dscores, k_item, preferred_element_type=jnp.float32
        ).astype(jnp.bfloat16)
        key_grad = jnp.einsum(
            "gmk,mgd->kd", dscores, q_item, preferred_element_type=jnp.float32
        ).astype(jnp.bfloat16)
        value_grad = jnp.einsum(
            "gmk,mgd->kd", probs_b, g_item, preferred_element_type=jnp.float32
        ).astype(jnp.bfloat16)
        query_parts.append(query_grad.reshape(query_in.shape[0], query_in.shape[1], group * HD))
        key_parts.append(key_grad.reshape(query_in.shape[0], query_in.shape[1], HD))
        value_parts.append(value_grad.reshape(query_in.shape[0], query_in.shape[1], HD))
    return (
        jnp.stack(query_parts, axis=2),
        jnp.stack(key_parts, axis=2),
        jnp.stack(value_parts, axis=2),
    )


def fetch_weight(value_weight):
    return lax.all_gather(value_weight, ("seq", "fsdp"), axis=0, tiled=True)


def body(inputs, queries, rotated_keys, out_grad, value_weight, fisher, anchor, doc_starts, owners):
    lane_count = lax.axis_size("seq")
    own_lane = lax.axis_index("seq")
    rounds = inputs.shape[1]
    capacity = 3 * rounds // (2 * lane_count)
    token_rows = inputs.reshape(rounds, inputs.shape[3])
    query_rows = queries.reshape(rounds, queries.shape[3])
    key_rows = rotated_keys.reshape(rounds, rotated_keys.shape[3])
    grad_rows = out_grad.reshape(rounds, out_grad.shape[3])
    doc_of, owner_of, rank_of = round_plan(doc_starts[0], owners[0], lane_count, rounds)
    source, filled = slot_rounds(owner_of, rank_of, lane_count, capacity)

    flat_slot = rank_of * lane_count + owner_of
    slot_ids = jnp.arange(capacity * lane_count, dtype=jnp.int32)
    select = (flat_slot[None, :] == slot_ids[:, None]).astype(jnp.bfloat16)

    def to_slots(rows):
        picked = jnp.dot(select, rows, preferred_element_type=jnp.float32).astype(jnp.bfloat16)
        return picked.reshape(capacity, lane_count, KVH, -1)

    token_cols = lax.all_to_all(
        token_rows.reshape(rounds, lane_count, -1), "seq", split_axis=1, concat_axis=1, tiled=True
    )

    query_send = to_slots(query_rows)
    grad_send = to_slots(grad_rows)
    key_send = to_slots(key_rows)
    my_rounds = lax.dynamic_index_in_dim(source, own_lane, 1, keepdims=False)
    my_filled = lax.dynamic_index_in_dim(filled, own_lane, 1, keepdims=False)
    lane_ids = jnp.arange(lane_count, dtype=jnp.int32)
    slot_pos = (my_rounds[:, None] * lane_count + lane_ids[None, :]).reshape(-1)
    round_doc = jnp.where(my_filled, jnp.take(doc_of, my_rounds), -1)
    slot_doc = jnp.broadcast_to(round_doc[:, None], (capacity, lane_count)).reshape(-1)
    slot_live = jnp.broadcast_to(my_filled[:, None], (capacity, lane_count)).reshape(-1)
    visible = (slot_doc[:, None] == slot_doc[None, :]) & (slot_pos[None, :] <= slot_pos[:, None])
    visible = visible & slot_live[:, None] & slot_live[None, :]
    full_weight = fetch_weight(value_weight)
    value_rows = jnp.dot(token_rows, full_weight, preferred_element_type=jnp.float32).astype(
        jnp.bfloat16
    )
    value_send = to_slots(value_rows)
    query_back, key_back, value_back = attend(
        lax.all_to_all(query_send, "seq", split_axis=1, concat_axis=1, tiled=True),
        lax.all_to_all(grad_send, "seq", split_axis=1, concat_axis=1, tiled=True),
        lax.all_to_all(key_send, "seq", split_axis=1, concat_axis=1, tiled=True),
        lax.all_to_all(value_send, "seq", split_axis=1, concat_axis=1, tiled=True),
        visible,
    )
    returned = (
        lax.all_to_all(key_back, "seq", split_axis=1, concat_axis=1, tiled=True),
        lax.all_to_all(value_back, "seq", split_axis=1, concat_axis=1, tiled=True),
    )
    def to_home(rows):
        flat = rows.reshape(capacity * lane_count, -1)
        return lax.dot_general(
            select, flat, (((0,), (0,)), ((), ())), preferred_element_type=jnp.float32
        ).astype(jnp.bfloat16)

    key_home = to_home(returned[0])
    value_home = to_home(returned[1])
    input_grad = jnp.einsum(
        "rk,dk->rd", value_home, full_weight, preferred_element_type=jnp.float32
    ).astype(jnp.bfloat16)
    all_values = lax.all_gather(value_home, "seq", axis=0, tiled=False)
    partial_sum = jnp.einsum(
        "rld,lrk->dk", token_cols, all_values, preferred_element_type=jnp.float32
    )
    summed = lax.psum_scatter(partial_sum, "fsdp", scatter_dimension=0, tiled=True)
    tokens_total = rounds * lane_count * lax.axis_size("fsdp")
    grad_scale = 1.0 / math.sqrt(tokens_total)
    ewc_grad = summed * grad_scale + EWC_LAMBDA * fisher * (
        value_weight.astype(jnp.float32) - anchor
    )
    query_out = query_back.reshape(1, 1, capacity, lane_count, -1)
    return (
        query_out,
        key_home.reshape(1, rounds, 1, -1),
        input_grad.reshape(1, rounds, 1, -1),
        ewc_grad,
    )


def solution(mesh):
    return jax.shard_map(
        body,
        mesh=mesh,
        in_specs=(
            P("fsdp", None, "seq", None),
            P("fsdp", None, "seq", None),
            P("fsdp", None, "seq", None),
            P("fsdp", None, "seq", None),
            P(("seq", "fsdp"), None),
            P(("seq", "fsdp"), None),
            P(("seq", "fsdp"), None),
            P("fsdp", None),
            P("fsdp", None),
        ),
        out_specs=(
            P("fsdp", "seq", None, None, None),
            P("fsdp", None, "seq", None),
            P("fsdp", None, "seq", None),
            P(("seq", "fsdp"), None),
        ),
        check_vma=False,
    )
```

```python
import functools
import math

import jax
import jax.numpy as jnp
from jax import lax
from jax.experimental import pallas as pl
from jax.experimental.pallas import tpu as pltpu
from jax.sharding import PartitionSpec as P

KVH = 4
HD = 128


SCORE_NEG = -1e30
EWC_LAMBDA = 4.0


def round_plan(starts, owner_list, lane_count, rounds):
    round_ids = jnp.arange(rounds, dtype=jnp.int32)
    start_rounds = starts // lane_count
    doc_of = jnp.sum((start_rounds[None, :] <= round_ids[:, None]).astype(jnp.int32), axis=1) - 1
    doc_ids = jnp.arange(starts.shape[0], dtype=jnp.int32)
    onehot = (doc_of[:, None] == doc_ids[None, :]).astype(jnp.int32)
    owner_of = jnp.sum(onehot * owner_list[None, :], axis=1)
    earlier = (owner_of[:, None] == owner_of[None, :]) & (round_ids[None, :] < round_ids[:, None])
    rank_of = jnp.sum(earlier.astype(jnp.int32), axis=1)
    return (doc_of, owner_of, rank_of)


def slot_rounds(owner_of, rank_of, lane_count, capacity):
    lane_ids = jnp.arange(lane_count, dtype=jnp.int32)
    slot_ids = jnp.arange(capacity, dtype=jnp.int32)
    round_ids = jnp.arange(owner_of.shape[0], dtype=jnp.int32)
    match = (owner_of[None, None, :] == lane_ids[None, :, None]) & (
        rank_of[None, None, :] == slot_ids[:, None, None]
    )
    source = jnp.sum(match.astype(jnp.int32) * round_ids[None, None, :], axis=2)
    filled = jnp.any(match, axis=2)
    return (source, filled)


def attend_kernel(lanes, capacity, q_ref, g_ref, kv_ref, vis_ref, dq_ref, dkv_ref):
    head = pl.program_id(0)
    slots = lanes * capacity
    scale = 1.0 / math.sqrt(HD)
    slot = lax.broadcasted_iota(jnp.int32, (slots, 1), 0)
    wanted = ((slot % lanes) * KVH + head) * capacity + slot // lanes
    columns = lax.broadcasted_iota(jnp.int32, (slots, slots * KVH), 1)
    pick = jnp.where(columns == wanted, 1.0, 0.0).astype(jnp.bfloat16)

    def dot(a, b, ca, cb):
        return lax.dot_general(
            a, b, (((ca,), (cb,)), ((), ())), preferred_element_type=jnp.float32
        )

    q_all = dot(pick, q_ref[...], 1, 0).astype(jnp.bfloat16)
    g_all = dot(pick, g_ref[...], 1, 0).astype(jnp.bfloat16)
    kv = dot(pick, kv_ref[...], 1, 0).astype(jnp.bfloat16)
    keys, values = kv[:, :HD], kv[:, HD:]
    visible = vis_ref[...] > 0.0
    key_sum = jnp.zeros((slots, HD), jnp.float32)
    value_sum = jnp.zeros((slots, HD), jnp.float32)
    for at in range(q_all.shape[1] // HD):
        q = q_all[:, at * HD : (at + 1) * HD]
        g = g_all[:, at * HD : (at + 1) * HD]
        masked = jnp.where(visible, dot(q, keys, 1, 1) * scale, SCORE_NEG)
        peak = jnp.max(masked, axis=1, keepdims=True)
        probs = jnp.where(visible, jnp.exp(masked - peak), 0.0)
        totals = jnp.sum(probs, axis=1, keepdims=True)
        probs = probs * (1.0 / jnp.where(totals > 0.0, totals, 1.0))
        probs_b = probs.astype(jnp.bfloat16)
        attn_out = dot(probs_b, values, 1, 0).astype(jnp.bfloat16)
        delta = jnp.sum(
            g.astype(jnp.float32) * attn_out.astype(jnp.float32), axis=1, keepdims=True
        )
        dprobs = dot(g, values, 1, 1)
        dscores = (probs * (dprobs - delta) * scale).astype(jnp.bfloat16)
        dq_ref[:, at * HD : (at + 1) * HD] = dot(dscores, keys, 1, 0).astype(jnp.bfloat16)
        key_sum = key_sum + dot(dscores, q, 0, 0)
        value_sum = value_sum + dot(probs_b, g, 0, 0)
    both = jnp.concatenate([key_sum, value_sum], axis=1).astype(jnp.bfloat16)
    placed = dot(pick, both, 0, 0).astype(jnp.bfloat16)

    @pl.when(head == 0)
    def _():
        dkv_ref[...] = placed

    @pl.when(head > 0)
    def _():
        dkv_ref[...] = dkv_ref[...] + placed


def attend(query_in, grad_in, kv_in, visible, lanes, capacity):
    slots = lanes * capacity
    rows, width = query_in.shape
    whole = lambda h: (0, 0)
    flops = 2 * slots * slots * width * KVH * 6 + 4 * rows * slots * width * KVH
    return pl.pallas_call(
        functools.partial(attend_kernel, lanes, capacity),
        grid=(KVH,),
        in_specs=[
            pl.BlockSpec((rows, width), whole),
            pl.BlockSpec((rows, width), whole),
            pl.BlockSpec((rows, 2 * HD), whole),
            pl.BlockSpec((slots, slots), whole),
        ],
        out_specs=[
            pl.BlockSpec((slots, width), lambda h: (0, h)),
            pl.BlockSpec((rows, 2 * HD), whole),
        ],
        out_shape=[
            jax.ShapeDtypeStruct((slots, width * KVH), jnp.bfloat16),
            jax.ShapeDtypeStruct((rows, 2 * HD), jnp.bfloat16),
        ],
        compiler_params=pltpu.CompilerParams(vmem_limit_bytes=40 * 1024 * 1024),
        cost_estimate=pl.CostEstimate(
            flops=flops,
            bytes_accessed=6 * rows * width,
            transcendentals=slots * slots * width * KVH // HD,
        ),
    )(query_in, grad_in, kv_in, visible)


def fetch_weight(value_weight):
    return lax.all_gather(value_weight, ("seq", "fsdp"), axis=0, tiled=True)


def body(inputs, queries, rotated_keys, out_grad, value_weight, fisher, anchor, doc_starts, owners):
    lane_count = lax.axis_size("seq")
    own_lane = lax.axis_index("seq")
    rounds = inputs.shape[1]
    capacity = 3 * rounds // (2 * lane_count)
    token_rows = inputs.reshape(rounds, inputs.shape[3])
    query_rows = queries.reshape(rounds, queries.shape[3])
    key_rows = rotated_keys.reshape(rounds, rotated_keys.shape[3])
    grad_rows = out_grad.reshape(rounds, out_grad.shape[3])
    doc_of, owner_of, rank_of = round_plan(doc_starts[0], owners[0], lane_count, rounds)
    source, filled = slot_rounds(owner_of, rank_of, lane_count, capacity)

    per_lane = KVH * capacity
    round_row = (owner_of[None, :] * KVH + jnp.arange(KVH, dtype=jnp.int32)[:, None]) * capacity
    round_row = (round_row + rank_of[None, :]).reshape(-1)
    row_ids = jnp.arange(lane_count * per_lane, dtype=jnp.int32)
    select = (row_ids[:, None] == round_row[None, :]).astype(jnp.bfloat16)

    def stacked(rows):
        width = rows.shape[1] // KVH
        return jnp.concatenate([rows[:, h * width : (h + 1) * width] for h in range(KVH)], axis=0)

    def exchange(rows):
        parts = rows.reshape(lane_count, per_lane, -1)
        moved = lax.all_to_all(parts, "seq", split_axis=0, concat_axis=0, tiled=True)
        return moved.reshape(lane_count * per_lane, -1)

    def to_owners(rows):
        return exchange(
            jnp.dot(select, rows, preferred_element_type=jnp.float32).astype(jnp.bfloat16)
        )

    full_weight = fetch_weight(value_weight)
    query_in = to_owners(stacked(query_rows))
    grad_in = to_owners(stacked(grad_rows))
    my_rounds = lax.dynamic_index_in_dim(source, own_lane, 1, keepdims=False)
    my_filled = lax.dynamic_index_in_dim(filled, own_lane, 1, keepdims=False)
    lane_ids = jnp.arange(lane_count, dtype=jnp.int32)
    slot_pos = (my_rounds[:, None] * lane_count + lane_ids[None, :]).reshape(-1)
    round_doc = jnp.where(my_filled, jnp.take(doc_of, my_rounds), -1)
    slot_doc = jnp.broadcast_to(round_doc[:, None], (capacity, lane_count)).reshape(-1)
    slot_live = jnp.broadcast_to(my_filled[:, None], (capacity, lane_count)).reshape(-1)
    visible = (slot_doc[:, None] == slot_doc[None, :]) & (slot_pos[None, :] <= slot_pos[:, None])
    visible = visible & slot_live[:, None] & slot_live[None, :]
    value_rows = jnp.dot(token_rows, full_weight, preferred_element_type=jnp.float32).astype(
        jnp.bfloat16
    )
    kv_in = to_owners(jnp.concatenate([stacked(key_rows), stacked(value_rows)], axis=1))
    kv_in, grad_in, later_rows = lax.optimization_barrier((kv_in, grad_in, token_rows))
    token_cols = lax.all_to_all(
        later_rows.reshape(rounds, lane_count, -1), "seq", split_axis=1, concat_axis=1, tiled=True
    )
    query_back, kv_back = attend(
        query_in, grad_in, kv_in, visible.astype(jnp.float32), lane_count, capacity
    )
    home = lax.dot_general(
        select, exchange(kv_back), (((0,), (0,)), ((), ())), preferred_element_type=jnp.float32
    ).astype(jnp.bfloat16)
    pieces = [home[h * rounds : (h + 1) * rounds] for h in range(KVH)]
    key_home = jnp.concatenate([piece[:, :HD] for piece in pieces], axis=1)
    value_home = jnp.concatenate([piece[:, HD:] for piece in pieces], axis=1)
    input_grad = jnp.einsum(
        "rk,dk->rd", value_home, full_weight, preferred_element_type=jnp.float32
    ).astype(jnp.bfloat16)
    all_values = lax.all_gather(value_home, "seq", axis=0, tiled=False)
    partial_sum = jnp.einsum(
        "rld,lrk->dk", token_cols, all_values, preferred_element_type=jnp.float32
    )
    summed = lax.psum_scatter(partial_sum, "fsdp", scatter_dimension=0, tiled=True)
    tokens_total = rounds * lane_count * lax.axis_size("fsdp")
    grad_scale = 1.0 / math.sqrt(tokens_total)
    ewc_grad = summed * grad_scale + EWC_LAMBDA * fisher * (
        value_weight.astype(jnp.float32) - anchor
    )
    query_out = query_back.reshape(1, 1, capacity, lane_count, -1)
    return (
        query_out,
        key_home.reshape(1, rounds, 1, -1),
        input_grad.reshape(1, rounds, 1, -1),
        ewc_grad,
    )


def solution(mesh):
    return jax.shard_map(
        body,
        mesh=mesh,
        in_specs=(
            P("fsdp", None, "seq", None),
            P("fsdp", None, "seq", None),
            P("fsdp", None, "seq", None),
            P("fsdp", None, "seq", None),
            P(("seq", "fsdp"), None),
            P(("seq", "fsdp"), None),
            P(("seq", "fsdp"), None),
            P("fsdp", None),
            P("fsdp", None),
        ),
        out_specs=(
            P("fsdp", "seq", None, None, None),
            P("fsdp", None, "seq", None),
            P("fsdp", None, "seq", None),
            P(("seq", "fsdp"), None),
        ),
        check_vma=False,
    )
```

```python
import functools
import math

import jax
import jax.numpy as jnp
from jax import lax
from jax.experimental import pallas as pl
from jax.experimental.pallas import tpu as pltpu
from jax.sharding import PartitionSpec as P

KVH = 4
HD = 128


SCORE_NEG = -1e30
EWC_LAMBDA = 4.0


def round_plan(starts, owner_list, lane_count, rounds):
    round_ids = jnp.arange(rounds, dtype=jnp.int32)
    start_rounds = starts // lane_count
    doc_of = jnp.sum((start_rounds[None, :] <= round_ids[:, None]).astype(jnp.int32), axis=1) - 1
    doc_ids = jnp.arange(starts.shape[0], dtype=jnp.int32)
    onehot = (doc_of[:, None] == doc_ids[None, :]).astype(jnp.int32)
    owner_of = jnp.sum(onehot * owner_list[None, :], axis=1)
    earlier = (owner_of[:, None] == owner_of[None, :]) & (round_ids[None, :] < round_ids[:, None])
    rank_of = jnp.sum(earlier.astype(jnp.int32), axis=1)
    return (doc_of, owner_of, rank_of)


def slot_rounds(owner_of, rank_of, lane_count, capacity):
    lane_ids = jnp.arange(lane_count, dtype=jnp.int32)
    slot_ids = jnp.arange(capacity, dtype=jnp.int32)
    round_ids = jnp.arange(owner_of.shape[0], dtype=jnp.int32)
    match = (owner_of[None, None, :] == lane_ids[None, :, None]) & (
        rank_of[None, None, :] == slot_ids[:, None, None]
    )
    source = jnp.sum(match.astype(jnp.int32) * round_ids[None, None, :], axis=2)
    filled = jnp.any(match, axis=2)
    return (source, filled)


def attend_kernel(lanes, capacity, q_ref, g_ref, kv_ref, vis_ref, dq_ref, dkv_ref):
    head = pl.program_id(0)
    slots = lanes * capacity
    scale = 1.0 / math.sqrt(HD)
    slot = lax.broadcasted_iota(jnp.int32, (slots, 1), 0)
    wanted = ((slot % lanes) * KVH + head) * capacity + slot // lanes
    columns = lax.broadcasted_iota(jnp.int32, (slots, slots * KVH), 1)
    pick = jnp.where(columns == wanted, 1.0, 0.0).astype(jnp.bfloat16)

    def dot(a, b, ca, cb):
        return lax.dot_general(
            a, b, (((ca,), (cb,)), ((), ())), preferred_element_type=jnp.float32
        )

    q_all = dot(pick, q_ref[...], 1, 0).astype(jnp.bfloat16)
    g_all = dot(pick, g_ref[...], 1, 0).astype(jnp.bfloat16)
    kv = dot(pick, kv_ref[...], 1, 0).astype(jnp.bfloat16)
    keys, values = kv[:, :HD], kv[:, HD:]
    visible = vis_ref[...] > 0.0
    key_sum = jnp.zeros((slots, HD), jnp.float32)
    value_sum = jnp.zeros((slots, HD), jnp.float32)
    for at in range(q_all.shape[1] // HD):
        q = q_all[:, at * HD : (at + 1) * HD]
        g = g_all[:, at * HD : (at + 1) * HD]
        masked = jnp.where(visible, dot(q, keys, 1, 1) * scale, SCORE_NEG)
        peak = jnp.max(masked, axis=1, keepdims=True)
        probs = jnp.where(visible, jnp.exp(masked - peak), 0.0)
        totals = jnp.sum(probs, axis=1, keepdims=True)
        probs = probs * (1.0 / jnp.where(totals > 0.0, totals, 1.0))
        probs_b = probs.astype(jnp.bfloat16)
        attn_out = dot(probs_b, values, 1, 0).astype(jnp.bfloat16)
        delta = jnp.sum(
            g.astype(jnp.float32) * attn_out.astype(jnp.float32), axis=1, keepdims=True
        )
        dprobs = dot(g, values, 1, 1)
        dscores = (probs * (dprobs - delta) * scale).astype(jnp.bfloat16)
        dq_ref[:, at * HD : (at + 1) * HD] = dot(dscores, keys, 1, 0).astype(jnp.bfloat16)
        key_sum = key_sum + dot(dscores, q, 0, 0)
        value_sum = value_sum + dot(probs_b, g, 0, 0)
    both = jnp.concatenate([key_sum, value_sum], axis=1).astype(jnp.bfloat16)
    placed = dot(pick, both, 0, 0).astype(jnp.bfloat16)

    @pl.when(head == 0)
    def _():
        dkv_ref[...] = placed

    @pl.when(head > 0)
    def _():
        dkv_ref[...] = dkv_ref[...] + placed


def attend(query_in, grad_in, kv_in, visible, lanes, capacity):
    slots = lanes * capacity
    rows, width = query_in.shape
    whole = lambda h: (0, 0)
    flops = 2 * slots * slots * width * KVH * 6 + 4 * rows * slots * width * KVH
    return pl.pallas_call(
        functools.partial(attend_kernel, lanes, capacity),
        grid=(KVH,),
        in_specs=[
            pl.BlockSpec((rows, width), whole),
            pl.BlockSpec((rows, width), whole),
            pl.BlockSpec((rows, 2 * HD), whole),
            pl.BlockSpec((slots, slots), whole),
        ],
        out_specs=[
            pl.BlockSpec((slots, width), lambda h: (0, h)),
            pl.BlockSpec((rows, 2 * HD), whole),
        ],
        out_shape=[
            jax.ShapeDtypeStruct((slots, width * KVH), jnp.bfloat16),
            jax.ShapeDtypeStruct((rows, 2 * HD), jnp.bfloat16),
        ],
        compiler_params=pltpu.CompilerParams(vmem_limit_bytes=40 * 1024 * 1024),
        cost_estimate=pl.CostEstimate(
            flops=flops,
            bytes_accessed=6 * rows * width,
            transcendentals=slots * slots * width * KVH // HD,
        ),
    )(query_in, grad_in, kv_in, visible)


def lane_products(token_cols, value_home, lane_count, own_lane):
    steps = []
    step = lane_count // 2
    while step >= 1:
        steps.append(step)
        step //= 2
    offsets = [0]
    for step in steps:
        offsets = offsets + [at ^ step for at in offsets]
    ordered = jnp.concatenate(
        [lax.dynamic_slice_in_dim(token_cols, own_lane ^ at, 1, 0) for at in offsets], axis=0
    )

    def product(first, values):
        tokens = ordered[first : first + values.shape[0]].reshape(-1, ordered.shape[2])
        return lax.dot_general(
            tokens,
            values.reshape(-1, values.shape[2]),
            (((0,), (0,)), ((), ())),
            preferred_element_type=jnp.float32,
        )

    held = value_home[None]
    total = product(0, held)
    for step in steps:
        pairs = [(lane, lane ^ step) for lane in range(lane_count)]
        arrived = lax.ppermute(held, "seq", pairs)
        total = total + product(held.shape[0], arrived)
        if step > 1:
            held = jnp.concatenate([held, arrived], axis=0)
    return total


def sum_rows(partial_sum):
    count = lax.axis_size("fsdp")
    own = lax.axis_index("fsdp")
    rows = partial_sum.shape[0] // count
    total = lax.dynamic_slice_in_dim(partial_sum, own * rows, rows, 0)
    for shift in range(1, count):
        target = (own + shift) % count
        part = lax.dynamic_slice_in_dim(partial_sum, target * rows, rows, 0)
        pairs = [(at, (at + shift) % count) for at in range(count)]
        total = total + lax.ppermute(part, "fsdp", pairs)
    return total


def fetch_weight(value_weight):
    return lax.all_gather(value_weight, ("seq", "fsdp"), axis=0, tiled=True)


def body(inputs, queries, rotated_keys, out_grad, value_weight, fisher, anchor, doc_starts, owners):
    lane_count = lax.axis_size("seq")
    own_lane = lax.axis_index("seq")
    rounds = inputs.shape[1]
    capacity = 3 * rounds // (2 * lane_count)
    token_rows = inputs.reshape(rounds, inputs.shape[3])
    query_rows = queries.reshape(rounds, queries.shape[3])
    key_rows = rotated_keys.reshape(rounds, rotated_keys.shape[3])
    grad_rows = out_grad.reshape(rounds, out_grad.shape[3])
    doc_of, owner_of, rank_of = round_plan(doc_starts[0], owners[0], lane_count, rounds)
    source, filled = slot_rounds(owner_of, rank_of, lane_count, capacity)

    per_lane = KVH * capacity
    round_row = (owner_of[None, :] * KVH + jnp.arange(KVH, dtype=jnp.int32)[:, None]) * capacity
    round_row = (round_row + rank_of[None, :]).reshape(-1)
    row_ids = jnp.arange(lane_count * per_lane, dtype=jnp.int32)
    select = (row_ids[:, None] == round_row[None, :]).astype(jnp.bfloat16)

    def stacked(rows):
        width = rows.shape[1] // KVH
        return jnp.concatenate([rows[:, h * width : (h + 1) * width] for h in range(KVH)], axis=0)

    def exchange(rows):
        parts = rows.reshape(lane_count, per_lane, -1)
        moved = lax.all_to_all(parts, "seq", split_axis=0, concat_axis=0, tiled=True)
        return moved.reshape(lane_count * per_lane, -1)

    def to_owners(rows):
        return exchange(
            jnp.dot(select, rows, preferred_element_type=jnp.float32).astype(jnp.bfloat16)
        )

    full_weight = fetch_weight(value_weight)
    query_in = to_owners(stacked(query_rows))
    grad_in = to_owners(stacked(grad_rows))
    my_rounds = lax.dynamic_index_in_dim(source, own_lane, 1, keepdims=False)
    my_filled = lax.dynamic_index_in_dim(filled, own_lane, 1, keepdims=False)
    lane_ids = jnp.arange(lane_count, dtype=jnp.int32)
    slot_pos = (my_rounds[:, None] * lane_count + lane_ids[None, :]).reshape(-1)
    round_doc = jnp.where(my_filled, jnp.take(doc_of, my_rounds), -1)
    slot_doc = jnp.broadcast_to(round_doc[:, None], (capacity, lane_count)).reshape(-1)
    slot_live = jnp.broadcast_to(my_filled[:, None], (capacity, lane_count)).reshape(-1)
    visible = (slot_doc[:, None] == slot_doc[None, :]) & (slot_pos[None, :] <= slot_pos[:, None])
    visible = visible & slot_live[:, None] & slot_live[None, :]
    value_tokens, query_in, grad_in = lax.optimization_barrier((token_rows, query_in, grad_in))
    value_rows = jnp.dot(value_tokens, full_weight, preferred_element_type=jnp.float32).astype(
        jnp.bfloat16
    )
    kv_in = to_owners(jnp.concatenate([stacked(key_rows), stacked(value_rows)], axis=1))
    kv_in, grad_in, later_rows = lax.optimization_barrier((kv_in, grad_in, token_rows))
    token_cols = lax.all_to_all(
        later_rows.reshape(rounds, lane_count, -1).transpose(1, 0, 2),
        "seq",
        split_axis=0,
        concat_axis=0,
        tiled=True,
    )
    query_back, kv_back = attend(
        query_in, grad_in, kv_in, visible.astype(jnp.float32), lane_count, capacity
    )
    kv_back, token_cols = lax.optimization_barrier((kv_back, token_cols))
    home = lax.dot_general(
        select, exchange(kv_back), (((0,), (0,)), ((), ())), preferred_element_type=jnp.float32
    ).astype(jnp.bfloat16)
    pieces = [home[h * rounds : (h + 1) * rounds] for h in range(KVH)]
    key_home = jnp.concatenate([piece[:, :HD] for piece in pieces], axis=1)
    value_home = jnp.concatenate([piece[:, HD:] for piece in pieces], axis=1)
    input_grad = jnp.einsum(
        "rk,dk->rd", value_home, full_weight, preferred_element_type=jnp.float32
    ).astype(jnp.bfloat16)
    partial_sum = lane_products(token_cols, value_home, lane_count, own_lane)
    summed = sum_rows(partial_sum)
    tokens_total = rounds * lane_count * lax.axis_size("fsdp")
    grad_scale = 1.0 / math.sqrt(tokens_total)
    ewc_grad = summed * grad_scale + EWC_LAMBDA * fisher * (
        value_weight.astype(jnp.float32) - anchor
    )
    query_out = query_back.reshape(1, 1, capacity, lane_count, -1)
    return (
        query_out,
        key_home.reshape(1, rounds, 1, -1),
        input_grad.reshape(1, rounds, 1, -1),
        ewc_grad,
    )


def solution(mesh):
    return jax.shard_map(
        body,
        mesh=mesh,
        in_specs=(
            P("fsdp", None, "seq", None),
            P("fsdp", None, "seq", None),
            P("fsdp", None, "seq", None),
            P("fsdp", None, "seq", None),
            P(("seq", "fsdp"), None),
            P(("seq", "fsdp"), None),
            P(("seq", "fsdp"), None),
            P("fsdp", None),
            P("fsdp", None),
        ),
        out_specs=(
            P("fsdp", "seq", None, None, None),
            P("fsdp", None, "seq", None),
            P("fsdp", None, "seq", None),
            P(("seq", "fsdp"), None),
        ),
        check_vma=False,
    )
```
